32 devices in a mesh: ctx: 32 (over z, y, x, core), head: 1.
Axes of the slice: x: 2, y: 2, z: 4, core: 2. Of those that a mesh axis runs over, the one named last changes fastest.
Arguments:
- queries: bfloat16 [4096, 4096], P('ctx', 'head'), may hold values from -9 to 9
- key_rows: bfloat16 [4096, 4096], P('ctx', 'head'), may hold values from -9 to 9
- value_rows: bfloat16 [4096, 4096], P('ctx', 'head'), may hold values from -6 to 6
- offsets: int32 [3, 32], P(None, 'head'), may hold values from 0 to 3, as said below
- sublayer_norm_gain: float32 [4096], P('head'), may hold values from 0.25 to 1.75
- cotangent: bfloat16 [4096, 4096], P('ctx', 'head'), may hold values from -6 to 6
Outputs:
- normed: bfloat16 [4096, 4096], P('ctx', 'head')
- query_grad: bfloat16 [4096, 4096], P('ctx', 'head')
- key_grad: bfloat16 [4096, 4096], P('ctx', 'head')
- value_grad: bfloat16 [4096, 4096], P('ctx', 'head')
The draws below stay inside these ranges and needn't reach their ends.
Inputs may be any that keep to these rules, and one draw needn't show every extreme that they name: Row l holds offsets of 0 to 2**l - 1, and each of these values belongs to exactly 32 / 2**l heads.
All inputs are finite; a program needn't handle non-finite values.
Results may differ from the reference program's by a relative error of at most 0.007.
Values may be sent and summed in bfloat16 or wider, within the bound.
A program may use at most 192 MiB of HBM per device.

```python
import math
from functools import reduce
import jax
import jax.numpy as jnp
from jax import lax

HEADS = 32
HD = 128
SEG0 = 512
LEVELS = 3
TOKENS = 4096
FEATURES = 4096


def draw_pair(key):
    base = jax.random.fold_in(key, 11)
    key_query, key_keys = jax.random.split(base, 2)
    shape3 = (TOKENS, HEADS, HD)
    query_vals = jnp.clip(jax.random.normal(key_query, shape3, jnp.float32), -4.0, 4.0)
    keys_vals = jnp.clip(jax.random.normal(key_keys, shape3, jnp.float32), -4.0, 4.0)
    query_out = query_vals.reshape(TOKENS, HEADS * HD).astype(jnp.bfloat16)
    keys_out = keys_vals.reshape(TOKENS, HEADS * HD).astype(jnp.bfloat16)
    return (query_out, keys_out)


def draw_queries(key, part):
    return draw_pair(key)[0]


def draw_key_rows(key, part):
    return draw_pair(key)[1]


def draw_offsets(key, part):
    levels_out = []
    for level_num in range(LEVELS):
        sub_key = jax.random.fold_in(key, 100 + level_num)
        order = jax.random.permutation(sub_key, HEADS).astype(jnp.int32)
        shifted = jax.random.randint(jax.random.fold_in(sub_key, 1), (), 0, 2 ** level_num)
        levels_out.append((order + shifted) % 2 ** level_num)
    return jnp.stack(levels_out).astype(jnp.int32)


def level_of(stream_key, shape, cuts, least, high):
    def one(axis_at, blocks):
        steps = jax.random.uniform(jax.random.fold_in(jax.random.fold_in(stream_key, 6), axis_at), (blocks,), jnp.float32, least / len(cuts), high / len(cuts))
        return jnp.repeat(jnp.exp(steps), shape[axis_at] // blocks).reshape((-1,) + (1,) * (len(shape) - axis_at - 1))

    factor_of = one(*cuts[0])
    for cut in cuts[1:]:
        factor_of = factor_of * one(*cut)
    return factor_of


def scatter_about(rng, extent, width, bound, pieces=(), kind=jnp.bfloat16):
    entries = jax.random.normal(rng, extent, jnp.float32) * width
    if len(pieces) > 0:
        entries = level_of(rng, extent, pieces, -0.22, 0.18) * entries
    return jnp.clip(entries, min=-bound, max=bound).astype(kind)


def setup_inputs(seed: int = 0) -> dict:
    key_list = jax.random.split(jax.random.key(seed), 7)
    return {
        "queries": draw_queries(jax.random.fold_in(key_list[6], 71), 0),
        "key_rows": draw_key_rows(jax.random.fold_in(key_list[6], 71), 0),
        "value_rows": scatter_about(key_list[2], (TOKENS, FEATURES), 1.0, 6.0, ((0, 32),)),
        "offsets": draw_offsets(jax.random.fold_in(key_list[6], 71), 0),
        "sublayer_norm_gain": jnp.clip(1.0 + 0.15 * jax.random.normal(key_list[4], (FEATURES,), jnp.float32), 0.25, 1.75),
        "cotangent": scatter_about(key_list[5], (TOKENS, FEATURES), 1.0, 6.0, ((0, 32),)),
    }


NEG_FILL = -1e+30
EPSILON = 1e-05

def pick_rows(source, offset, stride):
    shaped = source.reshape((source.shape[0] // stride, stride) + source.shape[1:])
    return lax.dynamic_index_in_dim(shaped, offset, axis=1, keepdims=False)

def put_rows(picked, offset, stride, filler):
    count = picked.shape[0]
    chosen = jnp.arange(stride, dtype=jnp.int32) == offset
    chosen = chosen.reshape((1, stride) + (1,) * (picked.ndim - 1))
    spread = jnp.where(chosen, picked[:, None], jnp.asarray(filler, picked.dtype))
    return spread.reshape((count * stride,) + picked.shape[1:])

def round_trip(values):
    return lax.optimization_barrier(values.astype(jnp.bfloat16)).astype(jnp.float32)

def head_forward(operands):
    query_head, key_head, value_head, head_offsets = operands
    score_scale = 1.0 / math.sqrt(HD)
    maxima = []
    totals = []
    partials = []
    for level_num in range(LEVELS):
        stride = 2 ** level_num
        offset = head_offsets[level_num]
        query_sel = pick_rows(query_head, offset, stride).reshape(-1, SEG0, HD).astype(jnp.float32)
        key_sel = pick_rows(key_head, offset, stride).reshape(-1, SEG0, HD).astype(jnp.float32)
        value_sel = pick_rows(value_head, offset, stride).reshape(-1, SEG0, HD).astype(jnp.float32)
        scores = jnp.einsum('sqd,skd->sqk', query_sel, key_sel) * score_scale
        row_max = lax.optimization_barrier(jnp.max(scores, axis=-1))
        weights = jnp.exp(scores - row_max[..., None])
        row_total = lax.optimization_barrier(jnp.sum(weights, axis=-1))
        level_out = jnp.einsum('sqk,skd->sqd', round_trip(weights), value_sel)
        maxima.append(put_rows(row_max.reshape(-1), offset, stride, NEG_FILL))
        totals.append(put_rows(row_total.reshape(-1), offset, stride, 0.0))
        partials.append(put_rows(level_out.reshape(-1, HD), offset, stride, 0.0))
    top_max = reduce(jnp.maximum, maxima)
    factors = [jnp.exp(each_max - top_max) for each_max in maxima]
    total = factors[0] * totals[0]
    summed = factors[0][:, None] * partials[0]
    for level_num in range(1, LEVELS):
        total = total + factors[level_num] * totals[level_num]
        summed = summed + factors[level_num][:, None] * partials[level_num]
    attended = (summed / total[:, None]).astype(jnp.bfloat16)
    return (attended, top_max + jnp.log(total))

def head_backward(operands):
    query_head, key_head, value_head, dout_head, lse_head, delta_head, head_offsets = operands
    score_scale = 1.0 / math.sqrt(HD)
    query_acc = jnp.zeros((TOKENS, HD), jnp.float32)
    key_acc = jnp.zeros((TOKENS, HD), jnp.float32)
    value_acc = jnp.zeros((TOKENS, HD), jnp.float32)
    for level_num in range(LEVELS):
        stride = 2 ** level_num
        offset = head_offsets[level_num]
        query_sel = pick_rows(query_head, offset, stride).reshape(-1, SEG0, HD).astype(jnp.float32)
        key_sel = pick_rows(key_head, offset, stride).reshape(-1, SEG0, HD).astype(jnp.float32)
        value_sel = pick_rows(value_head, offset, stride).reshape(-1, SEG0, HD).astype(jnp.float32)
        dout_sel = pick_rows(dout_head, offset, stride).reshape(-1, SEG0, HD).astype(jnp.float32)
        lse_sel = pick_rows(lse_head, offset, stride).reshape(-1, SEG0)
        delta_sel = pick_rows(delta_head, offset, stride).reshape(-1, SEG0)
        scores = jnp.einsum('sqd,skd->sqk', query_sel, key_sel) * score_scale
        probs = jnp.exp(scores - lse_sel[..., None])
        value_part = jnp.einsum('sqk,sqd->skd', round_trip(probs), dout_sel)
        dprobs = jnp.einsum('sqd,skd->sqk', dout_sel, value_sel)
        dscores = round_trip(probs * (dprobs - delta_sel[..., None]))
        query_part = jnp.einsum('sqk,skd->sqd', dscores, key_sel) * score_scale
        key_part = jnp.einsum('sqk,sqd->skd', dscores, query_sel) * score_scale
        query_acc = query_acc + put_rows(query_part.reshape(-1, HD), offset, stride, 0.0)
        key_acc = key_acc + put_rows(key_part.reshape(-1, HD), offset, stride, 0.0)
        value_acc = value_acc + put_rows(value_part.reshape(-1, HD), offset, stride, 0.0)
    return (query_acc.astype(jnp.bfloat16), key_acc.astype(jnp.bfloat16), value_acc.astype(jnp.bfloat16))

def by_head(array):
    return array.reshape(TOKENS, HEADS, HD).transpose(1, 0, 2)

def from_heads(array):
    return array.transpose(1, 0, 2).reshape(TOKENS, HEADS * HD)

def reference(queries, key_rows, value_rows, offsets, sublayer_norm_gain, cotangent):
    feature_total_count = HEADS * HD
    query_heads = by_head(queries)
    key_heads = by_head(key_rows)
    value_heads = by_head(value_rows)
    head_offsets = offsets.T
    attended, log_total = lax.map(head_forward, (query_heads, key_heads, value_heads, head_offsets))
    attended_rows_flattened = from_heads(attended).astype(jnp.float32)
    feature_mean = lax.optimization_barrier(jnp.sum(attended_rows_flattened, axis=1)) / feature_total_count
    variance = lax.optimization_barrier(jnp.sum(attended_rows_flattened * attended_rows_flattened, axis=1)) / feature_total_count - feature_mean * feature_mean
    inverse_deviation = 1.0 / jnp.sqrt(variance + EPSILON)
    normalized_input = (attended_rows_flattened - feature_mean[:, None]) * inverse_deviation[:, None]
    normed = (normalized_input * sublayer_norm_gain[None, :]).astype(jnp.bfloat16)
    normalized_gradient = cotangent.astype(jnp.float32) * sublayer_norm_gain[None, :]
    gradient_sum_first = lax.optimization_barrier(jnp.sum(normalized_gradient, axis=1))
    gradient_sum_second = lax.optimization_barrier(jnp.sum(normalized_gradient * normalized_input, axis=1))
    attended_gradient = ((normalized_gradient - gradient_sum_first[:, None] / feature_total_count - normalized_input * gradient_sum_second[:, None] / feature_total_count) * inverse_deviation[:, None]).astype(jnp.bfloat16)
    dout_heads = by_head(attended_gradient)
    delta = lax.optimization_barrier(jnp.sum(dout_heads.astype(jnp.float32) * attended.astype(jnp.float32), axis=-1))
    grads = lax.map(head_backward, (query_heads, key_heads, value_heads, dout_heads, log_total, delta, head_offsets))
    return (normed, from_heads(grads[0]), from_heads(grads[1]), from_heads(grads[2]))
```

```python
import functools
import math

import jax
import jax.numpy as jnp
from jax import lax
from jax.experimental import pallas as pl
from jax.experimental.pallas import tpu as pltpu
from jax.sharding import PartitionSpec as P

SEG0 = 512
LEVELS = 3
HD = 128
RES = 2 ** (LEVELS - 1)
NEG_FILL = -1e30
EPSILON = 1e-05
LOG2E = math.log2(math.e)
SCALE = 1.0 / math.sqrt(HD)
F32 = jnp.float32
BF16 = jnp.bfloat16


def nn(a, b):
    return lax.dot_general(a, b, (((1,), (0,)), ((), ())), preferred_element_type=F32)


def nt(a, b):
    return lax.dot_general(a, b, (((1,), (1,)), ((), ())), preferred_element_type=F32)


def wait_bytes(ref, sem):
    pltpu.make_async_copy(ref, ref, sem).wait()


def kernel(
    G, NH, HPD, T, total_features,
    offs, gain, q_in, k_in, v_in, c_in,
    n_out, dq_out, dk_out, dv_out,
    stage, recv, recv_c, osta, rout, kT, vT, attT, doT, doN,
    o1, ml1, o2, ml2, dq1, dk1, dv1, dq2, dk2, dv2,
    lse, delta, srecv, tot,
    send_sem, recv_sem, osend_sem, orecv_sem, ssend_sem, srecv_sem,
):
    R = T // RES
    LEN = G * R
    NP = G * NH
    SRC0 = SEG0 // T
    W0 = SRC0 * R
    SEGS0 = G // SRC0
    ctx = lax.axis_index("ctx")
    hidx = lax.axis_index("head")
    mine = lax.rem(ctx, G)
    base = ctx - mine
    slot = hidx * G + mine

    barrier = pltpu.get_barrier_semaphore()

    def greet(i, c):
        peer = lax.rem(slot + i, NP)
        pl.semaphore_signal(
            barrier, inc=1,
            device_id={"ctx": base + lax.rem(peer, G), "head": peer // G},
            device_id_type=pl.DeviceIdType.MESH,
        )
        return c

    lax.fori_loop(1, NP, greet, 0)

    ia = lax.broadcasted_iota(jnp.int32, (T, T), 0)
    ib = lax.broadcasted_iota(jnp.int32, (T, T), 1)
    perm = jnp.where(ib == lax.rem(ia, R) * RES + ia // R, 1.0, 0.0).astype(BF16)
    perm_t = jnp.where(ia == lax.rem(ib, R) * RES + ib // R, 1.0, 0.0).astype(BF16)
    ja = lax.broadcasted_iota(jnp.int32, (HD, HD), 0)
    jb = lax.broadcasted_iota(jnp.int32, (HD, HD), 1)
    eye_mask = ja == jb
    eye = jnp.where(eye_mask, 1.0, 0.0).astype(BF16)

    F = HPD * HD

    def put_stage(a, ref):
        for d in range(G):
            y = nn(perm, ref[:, d * F:(d + 1) * F]).astype(BF16)
            for hh in range(HPD):
                stage[a, d, hh] = y[:, hh * HD:(hh + 1) * HD].reshape(RES, R, HD)

    def send_stage(a):
        into = recv.at[a] if a < 3 else recv_c

        def one(i, c):
            d = lax.rem(mine + i, G)
            pltpu.make_async_remote_copy(
                src_ref=stage.at[a, d],
                dst_ref=into.at[:, :, mine],
                send_sem=send_sem.at[a],
                recv_sem=recv_sem.at[a],
                device_id={"ctx": base + d},
                device_id_type=pl.DeviceIdType.MESH,
            ).start()
            return c

        lax.fori_loop(1, G, one, 0)
        into[:, :, mine] = stage[a, mine]

    put_stage(0, q_in)
    pl.semaphore_wait(barrier, NP - 1)
    send_stage(0)
    for a, ref in ((1, k_in), (2, v_in), (3, c_in)):
        put_stage(a, ref)
        send_stage(a)

    def offset(level, hh):
        if level == 0:
            return 0
        return offs[level, mine * HPD + hh]

    def n_pick(load, level, s, off):
        n = SRC0 << level
        parts = [
            load(off + (j << level), pl.ds(s * n, n)).reshape(n * R, HD)
            for j in range(RES >> level)
        ]
        return parts[0] if len(parts) == 1 else jnp.concatenate(parts, 0)

    def t_pick(load, level, s, off):
        w = W0 << level
        start = s * w if isinstance(s, int) else pl.multiple_of(s * w, w)
        parts = [load(off + (j << level), pl.ds(start, w)) for j in range(RES >> level)]
        return parts[0] if len(parts) == 1 else jnp.concatenate(parts, 1)

    for a in range(3):
        wait_bytes(recv.at[a, :, :, pl.ds(0, G - 1)], recv_sem.at[a])

    def rows(a, hh):
        return lambda r, d: recv[a, hh, r, d]

    def turn(x):
        return nt(eye, x).astype(BF16)

    def level1_at(s, r):
        return pl.multiple_of((r // 2) * (2 * W0) + lax.rem(s, 2) * W0, W0)

    def forward(hh, carry):
        for r in range(RES):
            kT[hh, r] = turn(recv[1, hh, r].reshape(LEN, HD))
            vT[r] = turn(recv[2, hh, r].reshape(LEN, HD))
        offsets = [offset(level, hh) for level in range(LEVELS)]

        def segment(level, s):
            off = offsets[level]
            qn = n_pick(rows(0, hh), level, s, off)
            kn = n_pick(rows(1, hh), level, s, off)
            vt = t_pick(lambda r, d: vT[r, :, d], level, s, off)
            st = nt(kn, qn) * (SCALE * LOG2E)
            top = jnp.max(st, axis=0, keepdims=True)
            p = jnp.exp2(st - top)
            return nn(vt, p.astype(BF16)), top, jnp.sum(p, axis=0, keepdims=True)

        o, m, l = segment(2, 0)
        o2[...] = o
        ml2[0] = m
        ml2[1] = l
        for s in range(2):
            o, m, l = segment(1, s)
            o1[s] = o
            ml1[s, 0] = m
            ml1[s, 1] = l

        def level0(s, c):
            o, m, l = segment(0, s)
            lanes2 = pl.ds(pl.multiple_of(s * W0, W0), W0)
            for r in range(RES):
                here = slice(r * W0, (r + 1) * W0)
                lanes1 = pl.ds(level1_at(s, r), W0)
                m0 = m[:, here]
                m1 = jnp.where(offsets[1] == r % 2, ml1[s // 2, 0, :, lanes1], NEG_FILL)
                m2 = jnp.where(offsets[2] == r, ml2[0, :, lanes2], NEG_FILL)
                top = jnp.maximum(m0, jnp.maximum(m1, m2))
                f0 = jnp.exp2(m0 - top)
                f1 = jnp.exp2(m1 - top)
                f2 = jnp.exp2(m2 - top)
                total = f0 * l[:, here] + f1 * ml1[s // 2, 1, :, lanes1] + f2 * ml2[1, :, lanes2]
                summed = f0 * o[:, here] + f1 * o1[s // 2, :, lanes1] + f2 * o2[:, lanes2]
                attT[hh, r, :, lanes2] = (summed / total).astype(BF16)
                lse[hh, r, :, lanes2] = top + jnp.log(total) * LOG2E
            return c

        lax.fori_loop(0, SEGS0, level0, 0)
        return carry

    lax.fori_loop(0, HPD, forward, 0)

    wait_bytes(recv_c.at[:, :, pl.ds(0, G - 1)], recv_sem.at[3])

    def gain_of(hh):
        g = gain[pl.ds(mine * HPD + hh, 1), :]
        return jnp.sum(jnp.where(eye_mask, g, 0.0), axis=1, keepdims=True)

    gains = [gain_of(hh) for hh in range(HPD)]
    for r in range(RES):
        sums = None
        for hh in range(HPD):
            a = attT[hh, r].astype(F32)
            cT = turn(recv_c[hh, r].reshape(LEN, HD))
            doT[hh, r] = cT
            dx = cT.astype(F32) * gains[hh]
            part = [jnp.sum(x, axis=0, keepdims=True) for x in (a, a * a, dx, dx * a)]
            sums = part if sums is None else [x + y for x, y in zip(sums, part)]
        for kind in range(4):
            srecv[slot, kind * RES + r] = sums[kind]

    def send_stats(i, c):
        peer = lax.rem(slot + i, NP)
        pltpu.make_async_remote_copy(
            src_ref=srecv.at[slot],
            dst_ref=srecv.at[slot],
            send_sem=ssend_sem,
            recv_sem=srecv_sem,
            device_id={"ctx": base + lax.rem(peer, G), "head": peer // G},
            device_id_type=pl.DeviceIdType.MESH,
        ).start()
        return c

    lax.fori_loop(1, NP, send_stats, 0)
    wait_bytes(srecv.at[pl.ds(0, NP - 1)], srecv_sem)
    tot[...] = jnp.sum(srecv[...], axis=0)

    inv_f = 1.0 / total_features
    for r in range(RES):
        mean = tot[r] * inv_f
        var = tot[RES + r] * inv_f - mean * mean
        inv = 1.0 / jnp.sqrt(var + EPSILON)
        s1 = tot[2 * RES + r]
        s2 = inv * (tot[3 * RES + r] - mean * s1)
        s1 = s1 * inv_f
        s2 = s2 * inv_f
        for hh in range(HPD):
            a = attT[hh, r].astype(F32)
            xhat = (a - mean) * inv
            normed = (xhat * gains[hh]).astype(BF16)
            dx = doT[hh, r].astype(F32) * gains[hh]
            d = ((dx - s1 - xhat * s2) * inv).astype(BF16)
            delta[hh, r] = jnp.sum(d.astype(F32) * a, axis=0, keepdims=True)
            doT[hh, r] = d
            n = SRC0
            for s in range(SEGS0):
                here = slice(s * W0, (s + 1) * W0)
                osta[0, hh, r, s * n:(s + 1) * n] = turn(normed[:, here]).reshape(n, R, HD)
                doN[hh, r, s * n:(s + 1) * n] = turn(d[:, here]).reshape(n, R, HD)

    def send_normed(i, c):
        d = lax.rem(mine + i, G)
        pltpu.make_async_remote_copy(
            src_ref=osta.at[0, :, :, d],
            dst_ref=rout.at[0, :, mine],
            send_sem=osend_sem.at[0],
            recv_sem=orecv_sem.at[0],
            device_id={"ctx": base + d},
            device_id_type=pl.DeviceIdType.MESH,
        ).start()
        return c

    lax.fori_loop(1, G, send_normed, 0)
    rout[0, :, mine] = osta[0, :, :, mine]

    def backward(hh, carry):
        offsets = [offset(level, hh) for level in range(LEVELS)]

        def segment(level, s):
            off = offsets[level]
            qn = n_pick(rows(0, hh), level, s, off)
            kn = n_pick(rows(1, hh), level, s, off)
            vn = n_pick(rows(2, hh), level, s, off)
            dn = n_pick(lambda r, d: doN[hh, r, d], level, s, off)
            dt = t_pick(lambda r, d: doT[hh, r, :, d], level, s, off)
            kt = t_pick(lambda r, d: kT[hh, r, :, d], level, s, off)
            ls = t_pick(lambda r, d: lse[hh, r, :, d], level, s, off)
            de = t_pick(lambda r, d: delta[hh, r, :, d], level, s, off)
            p = jnp.exp2(nt(kn, qn) * (SCALE * LOG2E) - ls)
            ds = (p * (nn(vn, dt) - de)).astype(BF16)
            return nn(kt, ds), nn(ds, qn), nn(p.astype(BF16), dn)

        dq2[...], dk2[...], dv2[...] = segment(2, 0)
        for s in range(2):
            dq1[s], dk1[s], dv1[s] = segment(1, s)
        w1 = [jnp.where(offsets[1] == r % 2, 1.0, 0.0).astype(F32) for r in range(RES)]
        w2 = [jnp.where(offsets[2] == r, 1.0, 0.0).astype(F32) for r in range(RES)]

        def level0(i, c):
            s = lax.rem(mine // SRC0 + i, SEGS0)
            dq, dk, dv = segment(0, s)
            at2 = pl.ds(pl.multiple_of(s * W0, W0), W0)
            to = pl.ds(s * SRC0, SRC0)
            for r in range(RES):
                here = slice(r * W0, (r + 1) * W0)
                at1 = pl.ds(level1_at(s, r), W0)
                x = (dq[:, here] + w1[r] * dq1[s // 2, :, at1] + w2[r] * dq2[:, at2]) * SCALE
                osta[1, hh, r, to] = turn(x.astype(BF16)).reshape(SRC0, R, HD)
                x = (dk[here] + w1[r] * dk1[s // 2, at1] + w2[r] * dk2[at2]) * SCALE
                osta[2, hh, r, to] = x.astype(BF16).reshape(SRC0, R, HD)
                x = dv[here] + w1[r] * dv1[s // 2, at1] + w2[r] * dv2[at2]
                osta[3, hh, r, to] = x.astype(BF16).reshape(SRC0, R, HD)
            for j in range(SRC0):
                d = s * SRC0 + j

                @pl.when(d != mine)
                def _():
                    pltpu.make_async_remote_copy(
                        src_ref=osta.at[pl.ds(1, 3), hh, :, d],
                        dst_ref=rout.at[pl.ds(1, 3), hh, mine],
                        send_sem=osend_sem.at[1 + hh],
                        recv_sem=orecv_sem.at[1 + hh],
                        device_id={"ctx": base + d},
                        device_id_type=pl.DeviceIdType.MESH,
                    ).start()

            return c

        lax.fori_loop(0, SEGS0, level0, 0)
        rout[pl.ds(1, 3), hh, mine] = osta[pl.ds(1, 3), hh, :, mine]
        return carry

    lax.fori_loop(0, HPD, backward, 0)

    def unpermute(ref, a, hh):
        for g in range(G):
            head = g * HPD + hh
            x = nn(perm_t, rout[a, hh, g].reshape(T, HD))
            ref[:, head * HD:(head + 1) * HD] = x.astype(BF16)

    wait_bytes(rout.at[0, :, pl.ds(0, G - 1)], orecv_sem.at[0])
    for hh in range(HPD):
        unpermute(n_out, 0, hh)
    for hh in range(HPD):
        wait_bytes(rout.at[pl.ds(1, 3), hh, pl.ds(0, G - 1)], orecv_sem.at[1 + hh])
        for a, ref in ((1, dq_out), (2, dk_out), (3, dv_out)):
            unpermute(ref, a, hh)

    for a in range(4):
        wait_bytes(stage.at[a, pl.ds(0, G - 1)], send_sem.at[a])
    wait_bytes(srecv.at[pl.ds(0, NP - 1)], ssend_sem)
    wait_bytes(osta.at[0, :, :, pl.ds(0, G - 1)], osend_sem.at[0])
    for hh in range(HPD):
        wait_bytes(osta.at[pl.ds(1, 3), hh, :, pl.ds(0, G - 1)], osend_sem.at[1 + hh])


def on_device(queries, key_rows, value_rows, offsets, sublayer_norm_gain, cotangent):
    T, features = queries.shape
    heads = offsets.shape[1]
    NH = lax.axis_size("head")
    G = SEG0 * RES // T
    HPD = heads // G
    R = T // RES
    LEN = G * R
    NP = G * NH
    vm = pl.BlockSpec(memory_space=pltpu.VMEM)
    out = jax.ShapeDtypeStruct((T, features), BF16)
    big = pltpu.VMEM((4, HPD, RES, G, R, HD), BF16)
    scratch = [
        pltpu.VMEM((4, G, HPD, RES, R, HD), BF16),
        pltpu.VMEM((3, HPD, RES, G, R, HD), BF16),
        pltpu.VMEM((HPD, RES, G, R, HD), BF16),
        big,
        pltpu.VMEM((4, HPD, G, RES, R, HD), BF16),
        pltpu.VMEM((HPD, RES, HD, LEN), BF16),
        pltpu.VMEM((RES, HD, LEN), BF16),
        pltpu.VMEM((HPD, RES, HD, LEN), BF16),
        pltpu.VMEM((HPD, RES, HD, LEN), BF16),
        pltpu.VMEM((HPD, RES, G, R, HD), BF16),
        pltpu.VMEM((2, HD, SEG0), F32),
        pltpu.VMEM((2, 2, 1, SEG0), F32),
        pltpu.VMEM((HD, SEG0), F32),
        pltpu.VMEM((2, 1, SEG0), F32),
        pltpu.VMEM((2, HD, SEG0), F32),
        pltpu.VMEM((2, SEG0, HD), F32),
        pltpu.VMEM((2, SEG0, HD), F32),
        pltpu.VMEM((HD, SEG0), F32),
        pltpu.VMEM((SEG0, HD), F32),
        pltpu.VMEM((SEG0, HD), F32),
        pltpu.VMEM((HPD, RES, 1, LEN), F32),
        pltpu.VMEM((HPD, RES, 1, LEN), F32),
        pltpu.VMEM((NP, 4 * RES, 1, LEN), F32),
        pltpu.VMEM((4 * RES, 1, LEN), F32),
        pltpu.SemaphoreType.DMA((4,)),
        pltpu.SemaphoreType.DMA((4,)),
        pltpu.SemaphoreType.DMA((1 + HPD,)),
        pltpu.SemaphoreType.DMA((1 + HPD,)),
        pltpu.SemaphoreType.DMA,
        pltpu.SemaphoreType.DMA,
    ]
    return pl.pallas_call(
        functools.partial(kernel, G, NH, HPD, T, float(NH * features)),
        out_shape=(out,) * 4,
        in_specs=[pl.BlockSpec(memory_space=pltpu.SMEM)] + [vm] * 5,
        out_specs=(vm,) * 4,
        scratch_shapes=scratch,
        compiler_params=pltpu.CompilerParams(
            collective_id=0, has_side_effects=True, vmem_limit_bytes=58 * 2**20
        ),
        cost_estimate=pl.CostEstimate(
            flops=7_000_000_000, bytes_accessed=8 * 2**20, transcendentals=8_000_000
        ),
    )(offsets, sublayer_norm_gain.reshape(heads, HD), queries, key_rows, value_rows, cotangent)


def solution(mesh):
    spec = P("ctx", "head")
    return jax.shard_map(
        on_device,
        mesh=mesh,
        in_specs=(spec, spec, spec, P(None, "head"), P("head"), spec),
        out_specs=(spec,) * 4,
        check_vma=False,
    )
```

```python
import functools
import math

import jax
import jax.numpy as jnp
from jax import lax
from jax.experimental import pallas as pl
from jax.experimental.pallas import tpu as pltpu
from jax.sharding import PartitionSpec as P

SEG0 = 512
LEVELS = 3
HD = 128
RES = 2 ** (LEVELS - 1)
NEG_FILL = -1e30
EPSILON = 1e-05
LOG2E = math.log2(math.e)
SCALE = 1.0 / math.sqrt(HD)
F32 = jnp.float32
BF16 = jnp.bfloat16


def nn(a, b):
    return lax.dot_general(a, b, (((1,), (0,)), ((), ())), preferred_element_type=F32)


def nt(a, b):
    return lax.dot_general(a, b, (((1,), (1,)), ((), ())), preferred_element_type=F32)


def wait_bytes(ref, sem):
    pltpu.make_async_copy(ref, ref, sem).wait()


def kernel(
    G, NH, HPD, T, total_features,
    offs, gain, q_in, k_in, v_in, c_in,
    rout, tot,
    xin, stage, recv, recv_c, osta, kT, vT, attT, doT, doN,
    o1, ml1, o2, ml2, dq1, dk1, dv1, dq2, dk2, dv2,
    lse, delta, srecv,
    in_sem, own_sem, send_sem, recv_sem, osend_sem, orecv_sem, ssend_sem, srecv_sem,
):
    R = T // RES
    LEN = G * R
    NP = G * NH
    SRC0 = SEG0 // T
    W0 = SRC0 * R
    SEGS0 = G // SRC0
    ctx = lax.axis_index("ctx")
    hidx = lax.axis_index("head")
    mine = lax.rem(ctx, G)
    base = ctx - mine
    slot = hidx * G + mine

    loads = [
        pltpu.make_async_copy(ref, xin.at[a], in_sem.at[a])
        for a, ref in enumerate((q_in, k_in, v_in, c_in))
    ]
    for load in loads:
        load.start()

    barrier = pltpu.get_barrier_semaphore()

    def greet(i, c):
        peer = lax.rem(slot + i, NP)
        pl.semaphore_signal(
            barrier, inc=1,
            device_id={"ctx": base + lax.rem(peer, G), "head": peer // G},
            device_id_type=pl.DeviceIdType.MESH,
        )
        return c

    lax.fori_loop(1, NP, greet, 0)

    ia = lax.broadcasted_iota(jnp.int32, (T, T), 0)
    ib = lax.broadcasted_iota(jnp.int32, (T, T), 1)
    perm = jnp.where(ib == lax.rem(ia, R) * RES + ia // R, 1.0, 0.0).astype(BF16)
    ja = lax.broadcasted_iota(jnp.int32, (HD, HD), 0)
    jb = lax.broadcasted_iota(jnp.int32, (HD, HD), 1)
    eye_mask = ja == jb
    eye = jnp.where(eye_mask, 1.0, 0.0).astype(BF16)

    F = HPD * HD

    def put_stage(a):
        loads[a].wait()
        for d in range(G):
            y = nn(perm, xin[a, :, d * F:(d + 1) * F]).astype(BF16)
            for hh in range(HPD):
                stage[a, d, hh] = y[:, hh * HD:(hh + 1) * HD].reshape(RES, R, HD)

    def send_stage(a):
        into = recv.at[a] if a < 3 else recv_c

        def one(i, c):
            d = lax.rem(mine + 7 * i, G)
            pltpu.make_async_remote_copy(
                src_ref=stage.at[a, d],
                dst_ref=into.at[:, :, mine],
                send_sem=send_sem.at[a],
                recv_sem=recv_sem.at[a],
                device_id={"ctx": base + d},
                device_id_type=pl.DeviceIdType.MESH,
            ).start()
            return c

        lax.fori_loop(1, G, one, 0)
        into[:, :, mine] = stage[a, mine]

    put_stage(0)
    pl.semaphore_wait(barrier, NP - 1)
    send_stage(0)
    for a in range(1, 4):
        put_stage(a)
        send_stage(a)

    def offset(level, hh):
        if level == 0:
            return 0
        return offs[level, mine * HPD + hh]

    def n_pick(load, level, s, off):
        n = SRC0 << level
        parts = [
            load(off + (j << level), pl.ds(s * n, n)).reshape(n * R, HD)
            for j in range(RES >> level)
        ]
        return parts[0] if len(parts) == 1 else jnp.concatenate(parts, 0)

    def t_pick(load, level, s, off):
        w = W0 << level
        start = s * w if isinstance(s, int) else pl.multiple_of(s * w, w)
        parts = [load(off + (j << level), pl.ds(start, w)) for j in range(RES >> level)]
        return parts[0] if len(parts) == 1 else jnp.concatenate(parts, 1)

    for a in range(3):
        wait_bytes(recv.at[a, :, :, pl.ds(0, G - 1)], recv_sem.at[a])

    def rows(a, hh):
        return lambda r, d: recv[a, hh, r, d]

    def turn(x):
        return nt(eye, x).astype(BF16)

    def level1_at(s, r):
        return pl.multiple_of((r // 2) * (2 * W0) + lax.rem(s, 2) * W0, W0)

    def forward(hh, carry):
        for r in range(RES):
            kT[hh, r] = turn(recv[1, hh, r].reshape(LEN, HD))
            vT[r] = turn(recv[2, hh, r].reshape(LEN, HD))
        offsets = [offset(level, hh) for level in range(LEVELS)]

        def segment(level, s):
            off = offsets[level]
            qn = n_pick(rows(0, hh), level, s, off)
            kn = n_pick(rows(1, hh), level, s, off)
            vt = t_pick(lambda r, d: vT[r, :, d], level, s, off)
            st = nt(kn, qn) * (SCALE * LOG2E)
            top = jnp.max(st, axis=0, keepdims=True)
            p = jnp.exp2(st - top)
            return nn(vt, p.astype(BF16)), top, jnp.sum(p, axis=0, keepdims=True)

        o, m, l = segment(2, 0)
        o2[...] = o
        ml2[0] = m
        ml2[1] = l
        for s in range(2):
            o, m, l = segment(1, s)
            o1[s] = o
            ml1[s, 0] = m
            ml1[s, 1] = l

        def level0(s, c):
            o, m, l = segment(0, s)
            lanes2 = pl.ds(pl.multiple_of(s * W0, W0), W0)
            for r in range(RES):
                here = slice(r * W0, (r + 1) * W0)
                lanes1 = pl.ds(level1_at(s, r), W0)
                m0 = m[:, here]
                m1 = jnp.where(offsets[1] == r % 2, ml1[s // 2, 0, :, lanes1], NEG_FILL)
                m2 = jnp.where(offsets[2] == r, ml2[0, :, lanes2], NEG_FILL)
                top = jnp.maximum(m0, jnp.maximum(m1, m2))
                f0 = jnp.exp2(m0 - top)
                f1 = jnp.exp2(m1 - top)
                f2 = jnp.exp2(m2 - top)
                total = f0 * l[:, here] + f1 * ml1[s // 2, 1, :, lanes1] + f2 * ml2[1, :, lanes2]
                summed = f0 * o[:, here] + f1 * o1[s // 2, :, lanes1] + f2 * o2[:, lanes2]
                att = (summed / total).astype(BF16)
                attT[hh, r, :, lanes2] = att
                osta[0, hh, r, pl.ds(s * SRC0, SRC0)] = turn(att).reshape(SRC0, R, HD)
                lse[hh, r, :, lanes2] = top + jnp.log(total) * LOG2E
            return c

        lax.fori_loop(0, SEGS0, level0, 0)
        return carry

    lax.fori_loop(0, HPD, forward, 0)

    wait_bytes(recv_c.at[:, :, pl.ds(0, G - 1)], recv_sem.at[3])

    def gain_of(hh):
        g = gain[pl.ds(mine * HPD + hh, 1), :]
        return jnp.sum(jnp.where(eye_mask, g, 0.0), axis=1, keepdims=True)

    gains = [gain_of(hh) for hh in range(HPD)]
    for r in range(RES):
        sums = None
        for hh in range(HPD):
            a = attT[hh, r].astype(F32)
            cT = turn(recv_c[hh, r].reshape(LEN, HD))
            doT[hh, r] = cT
            dx = cT.astype(F32) * gains[hh]
            part = [jnp.sum(x, axis=0, keepdims=True) for x in (a, a * a, dx, dx * a)]
            sums = part if sums is None else [x + y for x, y in zip(sums, part)]
        for kind in range(4):
            srecv[slot, kind * RES + r] = sums[kind]

    def send_stats(i, c):
        peer = lax.rem(slot + i, NP)
        pltpu.make_async_remote_copy(
            src_ref=srecv.at[slot],
            dst_ref=srecv.at[slot],
            send_sem=ssend_sem,
            recv_sem=srecv_sem,
            device_id={"ctx": base + lax.rem(peer, G), "head": peer // G},
            device_id_type=pl.DeviceIdType.MESH,
        ).start()
        return c

    lax.fori_loop(1, NP, send_stats, 0)

    def send_att(i, c):
        d = lax.rem(mine + 7 * i, G)
        pltpu.make_async_remote_copy(
            src_ref=osta.at[0, :, :, d],
            dst_ref=rout.at[0, :, mine],
            send_sem=osend_sem.at[0],
            recv_sem=orecv_sem.at[0],
            device_id={"ctx": base + d},
            device_id_type=pl.DeviceIdType.MESH,
        ).start()
        return c

    lax.fori_loop(1, G, send_att, 0)
    own_att = pltpu.make_async_copy(osta.at[0, :, :, mine], rout.at[0, :, mine], own_sem.at[HPD])
    own_att.start()

    wait_bytes(srecv.at[pl.ds(0, NP - 1)], srecv_sem)
    tot[...] = jnp.sum(srecv[...], axis=0)

    inv_f = 1.0 / total_features
    for r in range(RES):
        mean = tot[r] * inv_f
        var = tot[RES + r] * inv_f - mean * mean
        inv = 1.0 / jnp.sqrt(var + EPSILON)
        s1 = tot[2 * RES + r]
        s2 = inv * (tot[3 * RES + r] - mean * s1)
        s1 = s1 * inv_f
        s2 = s2 * inv_f
        for hh in range(HPD):
            a = attT[hh, r].astype(F32)
            xhat = (a - mean) * inv
            dx = doT[hh, r].astype(F32) * gains[hh]
            d = ((dx - s1 - xhat * s2) * inv).astype(BF16)
            delta[hh, r] = jnp.sum(d.astype(F32) * a, axis=0, keepdims=True)
            doT[hh, r] = d
            n = SRC0
            for s in range(SEGS0):
                here = slice(s * W0, (s + 1) * W0)
                doN[hh, r, s * n:(s + 1) * n] = turn(d[:, here]).reshape(n, R, HD)

    def backward(hh, carry):
        offsets = [offset(level, hh) for level in range(LEVELS)]

        def segment(level, s):
            off = offsets[level]
            qn = n_pick(rows(0, hh), level, s, off)
            kn = n_pick(rows(1, hh), level, s, off)
            vn = n_pick(rows(2, hh), level, s, off)
            dn = n_pick(lambda r, d: doN[hh, r, d], level, s, off)
            dt = t_pick(lambda r, d: doT[hh, r, :, d], level, s, off)
            kt = t_pick(lambda r, d: kT[hh, r, :, d], level, s, off)
            ls = t_pick(lambda r, d: lse[hh, r, :, d], level, s, off)
            de = t_pick(lambda r, d: delta[hh, r, :, d], level, s, off)
            p = jnp.exp2(nt(kn, qn) * (SCALE * LOG2E) - ls)
            ds = (p * (nn(vn, dt) - de)).astype(BF16)
            return nn(kt, ds), nn(ds, qn), nn(p.astype(BF16), dn)

        dq2[...], dk2[...], dv2[...] = segment(2, 0)
        for s in range(2):
            dq1[s], dk1[s], dv1[s] = segment(1, s)
        w1 = [jnp.where(offsets[1] == r % 2, 1.0, 0.0).astype(F32) for r in range(RES)]
        w2 = [jnp.where(offsets[2] == r, 1.0, 0.0).astype(F32) for r in range(RES)]

        def level0(s, c):
            dq, dk, dv = segment(0, s)
            at2 = pl.ds(pl.multiple_of(s * W0, W0), W0)
            to = pl.ds(s * SRC0, SRC0)
            for r in range(RES):
                here = slice(r * W0, (r + 1) * W0)
                at1 = pl.ds(level1_at(s, r), W0)
                x = (dq[:, here] + w1[r] * dq1[s // 2, :, at1] + w2[r] * dq2[:, at2]) * SCALE
                osta[1, hh, r, to] = turn(x.astype(BF16)).reshape(SRC0, R, HD)
                x = (dk[here] + w1[r] * dk1[s // 2, at1] + w2[r] * dk2[at2]) * SCALE
                osta[2, hh, r, to] = x.astype(BF16).reshape(SRC0, R, HD)
                x = dv[here] + w1[r] * dv1[s // 2, at1] + w2[r] * dv2[at2]
                osta[3, hh, r, to] = x.astype(BF16).reshape(SRC0, R, HD)
            return c

        lax.fori_loop(0, SEGS0, level0, 0)

        def send(i, c):
            d = lax.rem(mine + 7 * i, G)
            pltpu.make_async_remote_copy(
                src_ref=osta.at[pl.ds(1, 3), hh, :, d],
                dst_ref=rout.at[pl.ds(1, 3), hh, mine],
                send_sem=osend_sem.at[1 + hh],
                recv_sem=orecv_sem.at[1 + hh],
                device_id={"ctx": base + d},
                device_id_type=pl.DeviceIdType.MESH,
            ).start()
            return c

        lax.fori_loop(1, G, send, 0)
        pltpu.make_async_copy(
            osta.at[pl.ds(1, 3), hh, :, mine], rout.at[pl.ds(1, 3), hh, mine], own_sem.at[hh]
        ).start()
        return carry

    lax.fori_loop(0, HPD, backward, 0)

    wait_bytes(rout.at[0, :, pl.ds(0, G - 1)], orecv_sem.at[0])
    own_att.wait()
    for hh in range(HPD):
        wait_bytes(rout.at[pl.ds(1, 3), hh, pl.ds(0, G - 1)], orecv_sem.at[1 + hh])
        pltpu.make_async_copy(
            osta.at[pl.ds(1, 3), hh, :, mine], rout.at[pl.ds(1, 3), hh, mine], own_sem.at[hh]
        ).wait()

    for a in range(4):
        wait_bytes(stage.at[a, pl.ds(0, G - 1)], send_sem.at[a])
    wait_bytes(srecv.at[pl.ds(0, NP - 1)], ssend_sem)
    wait_bytes(osta.at[0, :, :, pl.ds(0, G - 1)], osend_sem.at[0])
    for hh in range(HPD):
        wait_bytes(osta.at[pl.ds(1, 3), hh, :, pl.ds(0, G - 1)], osend_sem.at[1 + hh])


def finish(G, HPD, T, total_features, rout, tot, gain, n_out, dq_out, dk_out, dv_out):
    R = T // RES
    LEN = G * R
    mine = lax.rem(lax.axis_index("ctx"), G)
    ia = lax.broadcasted_iota(jnp.int32, (T, T), 0)
    ib = lax.broadcasted_iota(jnp.int32, (T, T), 1)
    perm_t = jnp.where(ia == lax.rem(ib, R) * RES + ib // R, 1.0, 0.0).astype(BF16)
    row = lax.broadcasted_iota(jnp.int32, (R, LEN), 0)
    lane = lax.broadcasted_iota(jnp.int32, (R, LEN), 1)
    own = lane == mine * R + row

    def column(kind):
        parts = [
            jnp.sum(jnp.where(own, tot[kind * RES + r], 0.0), axis=1, keepdims=True)
            for r in range(RES)
        ]
        return jnp.concatenate(parts, 0)

    inv_f = 1.0 / total_features
    mean = column(0) * inv_f
    var = column(1) * inv_f - mean * mean
    inv = 1.0 / jnp.sqrt(var + EPSILON)
    for g in range(rout.shape[2]):
        for hh in range(HPD):
            head = g * HPD + hh
            here = slice(head * HD, (head + 1) * HD)
            a = rout[0, hh, g].reshape(T, HD).astype(F32)
            normed = ((a - mean) * inv * gain[:, here]).astype(BF16)
            n_out[:, here] = nn(perm_t, normed).astype(BF16)
            for k, ref in ((1, dq_out), (2, dk_out), (3, dv_out)):
                ref[:, here] = nn(perm_t, rout[k, hh, g].reshape(T, HD)).astype(BF16)


def on_device(queries, key_rows, value_rows, offsets, sublayer_norm_gain, cotangent):
    T, features = queries.shape
    heads = offsets.shape[1]
    NH = lax.axis_size("head")
    G = SEG0 * RES // T
    HPD = heads // G
    R = T // RES
    LEN = G * R
    NP = G * NH
    vm = pl.BlockSpec(memory_space=pltpu.VMEM)
    out = jax.ShapeDtypeStruct((T, features), BF16)
    big = pltpu.VMEM((4, HPD, RES, G, R, HD), BF16)
    scratch = [
        pltpu.VMEM((4, T, features), BF16),
        pltpu.VMEM((4, G, HPD, RES, R, HD), BF16),
        pltpu.VMEM((3, HPD, RES, G, R, HD), BF16),
        pltpu.VMEM((HPD, RES, G, R, HD), BF16),
        big,
        pltpu.VMEM((HPD, RES, HD, LEN), BF16),
        pltpu.VMEM((RES, HD, LEN), BF16),
        pltpu.VMEM((HPD, RES, HD, LEN), BF16),
        pltpu.VMEM((HPD, RES, HD, LEN), BF16),
        pltpu.VMEM((HPD, RES, G, R, HD), BF16),
        pltpu.VMEM((2, HD, SEG0), F32),
        pltpu.VMEM((2, 2, 1, SEG0), F32),
        pltpu.VMEM((HD, SEG0), F32),
        pltpu.VMEM((2, 1, SEG0), F32),
        pltpu.VMEM((2, HD, SEG0), F32),
        pltpu.VMEM((2, SEG0, HD), F32),
        pltpu.VMEM((2, SEG0, HD), F32),
        pltpu.VMEM((HD, SEG0), F32),
        pltpu.VMEM((SEG0, HD), F32),
        pltpu.VMEM((SEG0, HD), F32),
        pltpu.VMEM((HPD, RES, 1, LEN), F32),
        pltpu.VMEM((HPD, RES, 1, LEN), F32),
        pltpu.VMEM((NP, 4 * RES, 1, LEN), F32),
        pltpu.SemaphoreType.DMA((4,)),
        pltpu.SemaphoreType.DMA((1 + HPD,)),
        pltpu.SemaphoreType.DMA((4,)),
        pltpu.SemaphoreType.DMA((4,)),
        pltpu.SemaphoreType.DMA((1 + HPD,)),
        pltpu.SemaphoreType.DMA((1 + HPD,)),
        pltpu.SemaphoreType.DMA,
        pltpu.SemaphoreType.DMA,
    ]
    anywhere = pl.BlockSpec(memory_space=pl.ANY)
    total_features = float(NH * features)
    back, tot = pl.pallas_call(
        functools.partial(kernel, G, NH, HPD, T, total_features),
        out_shape=(
            jax.ShapeDtypeStruct((4, HPD, G, RES, R, HD), BF16),
            jax.ShapeDtypeStruct((4 * RES, 1, LEN), F32),
        ),
        in_specs=[pl.BlockSpec(memory_space=pltpu.SMEM), vm] + [anywhere] * 4,
        out_specs=(anywhere, vm),
        scratch_shapes=scratch,
        compiler_params=pltpu.CompilerParams(
            collective_id=0, has_side_effects=True, vmem_limit_bytes=58 * 2**20
        ),
        cost_estimate=pl.CostEstimate(
            flops=7_000_000_000, bytes_accessed=8 * 2**20, transcendentals=8_000_000
        ),
    )(offsets, sublayer_norm_gain.reshape(heads, HD), queries, key_rows, value_rows, cotangent)
    steps = min(4, G)
    width = features // steps
    return pl.pallas_call(
        functools.partial(finish, G, HPD, T, total_features),
        grid=(steps,),
        out_shape=(out,) * 4,
        in_specs=[
            pl.BlockSpec((4, HPD, G // steps, RES, R, HD), lambda i: (0, 0, i, 0, 0, 0)),
            pl.BlockSpec((4 * RES, 1, LEN), lambda i: (0, 0, 0)),
            pl.BlockSpec((1, width), lambda i: (0, i)),
        ],
        out_specs=(pl.BlockSpec((T, width), lambda i: (0, i)),) * 4,
        compiler_params=pltpu.CompilerParams(vmem_limit_bytes=58 * 2**20),
        cost_estimate=pl.CostEstimate(
            flops=8 * T * T * features, bytes_accessed=8 * 2**20, transcendentals=0
        ),
    )(back, tot, sublayer_norm_gain.reshape(1, features))


def solution(mesh):
    spec = P("ctx", "head")
    return jax.shard_map(
        on_device,
        mesh=mesh,
        in_specs=(spec, spec, spec, P(None, "head"), P("head"), spec),
        out_specs=(spec,) * 4,
        check_vma=False,
    )
```

```python
import functools
import math

import jax
import jax.numpy as jnp
from jax import lax
from jax.experimental import pallas as pl
from jax.experimental.pallas import tpu as pltpu
from jax.sharding import PartitionSpec as P

SEG0 = 512
LEVELS = 3
HD = 128
RES = 2 ** (LEVELS - 1)
NEG_FILL = -1e30
EPSILON = 1e-05
LOG2E = math.log2(math.e)
SCALE = 1.0 / math.sqrt(HD)
F32 = jnp.float32
BF16 = jnp.bfloat16


def nn(a, b):
    return lax.dot_general(a, b, (((1,), (0,)), ((), ())), preferred_element_type=F32)


def nt(a, b):
    return lax.dot_general(a, b, (((1,), (1,)), ((), ())), preferred_element_type=F32)


def wait_bytes(ref, sem):
    pltpu.make_async_copy(ref, ref, sem).wait()


def kernel(
    G, NH, HPD, T, total_features,
    offs, gain, q_in, k_in, v_in, c_in,
    rout, tot,
    xin, stage, recv, recv_c, osta, kT, vT, attT, doT, doN,
    o1, ml1, o2, ml2, dq1, dk1, dv1, dq2, dk2, dv2,
    lse, delta, part_sums, srecv, sums_all,
    in_sem, own_sem, send_sem, recv_sem, osend_sem, orecv_sem, ssend_sem, srecv_sem, gsend_sem, grecv_sem,
):
    R = T // RES
    LEN = G * R
    NP = G * NH
    SRC0 = SEG0 // T
    ROWS = 4 * RES // G
    W0 = SRC0 * R
    SEGS0 = G // SRC0
    ctx = lax.axis_index("ctx")
    hidx = lax.axis_index("head")
    mine = lax.rem(ctx, G)
    base = ctx - mine
    slot = hidx * G + mine

    loads = [
        pltpu.make_async_copy(ref, xin.at[a], in_sem.at[a])
        for a, ref in enumerate((q_in, k_in, v_in, c_in))
    ]
    for load in loads:
        load.start()

    barrier = pltpu.get_barrier_semaphore()

    def greet(i, c):
        peer = lax.rem(slot + i, NP)
        pl.semaphore_signal(
            barrier, inc=1,
            device_id={"ctx": base + lax.rem(peer, G), "head": peer // G},
            device_id_type=pl.DeviceIdType.MESH,
        )
        return c

    lax.fori_loop(1, NP, greet, 0)

    ia = lax.broadcasted_iota(jnp.int32, (T, T), 0)
    ib = lax.broadcasted_iota(jnp.int32, (T, T), 1)
    perm = jnp.where(ib == lax.rem(ia, R) * RES + ia // R, 1.0, 0.0).astype(BF16)
    ja = lax.broadcasted_iota(jnp.int32, (HD, HD), 0)
    jb = lax.broadcasted_iota(jnp.int32, (HD, HD), 1)
    eye_mask = ja == jb
    eye = jnp.where(eye_mask, 1.0, 0.0).astype(BF16)

    F = HPD * HD

    def put_stage(a):
        loads[a].wait()
        for d in range(G):
            y = nn(perm, xin[a, :, d * F:(d + 1) * F]).astype(BF16)
            for hh in range(HPD):
                stage[a, d, hh] = y[:, hh * HD:(hh + 1) * HD].reshape(RES, R, HD)

    def send_stage(a):
        into = recv.at[a] if a < 3 else recv_c

        def one(i, c):
            d = lax.rem(mine + 7 * i, G)
            pltpu.make_async_remote_copy(
                src_ref=stage.at[a, d],
                dst_ref=into.at[:, :, mine],
                send_sem=send_sem.at[a],
                recv_sem=recv_sem.at[a],
                device_id={"ctx": base + d},
                device_id_type=pl.DeviceIdType.MESH,
            ).start()
            return c

        lax.fori_loop(1, G, one, 0)
        into[:, :, mine] = stage[a, mine]

    put_stage(0)
    pl.semaphore_wait(barrier, NP - 1)
    send_stage(0)
    for a in range(1, 4):
        put_stage(a)
        send_stage(a)

    def offset(level, hh):
        if level == 0:
            return 0
        return offs[level, mine * HPD + hh]

    def n_pick(load, level, s, off):
        n = SRC0 << level
        parts = [
            load(off + (j << level), pl.ds(s * n, n)).reshape(n * R, HD)
            for j in range(RES >> level)
        ]
        return parts[0] if len(parts) == 1 else jnp.concatenate(parts, 0)

    def t_pick(load, level, s, off):
        w = W0 << level
        start = s * w if isinstance(s, int) else pl.multiple_of(s * w, w)
        parts = [load(off + (j << level), pl.ds(start, w)) for j in range(RES >> level)]
        return parts[0] if len(parts) == 1 else jnp.concatenate(parts, 1)

    for a in range(3):
        wait_bytes(recv.at[a, :, :, pl.ds(0, G - 1)], recv_sem.at[a])

    def rows(a, hh):
        return lambda r, d: recv[a, hh, r, d]

    def turn(x):
        return nt(eye, x).astype(BF16)

    def level1_at(s, r):
        return pl.multiple_of((r // 2) * (2 * W0) + lax.rem(s, 2) * W0, W0)

    def forward(hh, carry):
        for r in range(RES):
            kT[hh, r] = turn(recv[1, hh, r].reshape(LEN, HD))
            vT[r] = turn(recv[2, hh, r].reshape(LEN, HD))
        offsets = [offset(level, hh) for level in range(LEVELS)]

        def segment(level, s):
            off = offsets[level]
            qn = n_pick(rows(0, hh), level, s, off)
            kn = n_pick(rows(1, hh), level, s, off)
            vt = t_pick(lambda r, d: vT[r, :, d], level, s, off)
            st = nt(kn, qn) * (SCALE * LOG2E)
            top = jnp.max(st, axis=0, keepdims=True)
            p = jnp.exp2(st - top)
            return nn(vt, p.astype(BF16)), top, jnp.sum(p, axis=0, keepdims=True)

        o, m, l = segment(2, 0)
        o2[...] = o
        ml2[0] = m
        ml2[1] = l
        for s in range(2):
            o, m, l = segment(1, s)
            o1[s] = o
            ml1[s, 0] = m
            ml1[s, 1] = l

        def level0(s, c):
            o, m, l = segment(0, s)
            lanes2 = pl.ds(pl.multiple_of(s * W0, W0), W0)
            for r in range(RES):
                here = slice(r * W0, (r + 1) * W0)
                lanes1 = pl.ds(level1_at(s, r), W0)
                m0 = m[:, here]
                m1 = jnp.where(offsets[1] == r % 2, ml1[s // 2, 0, :, lanes1], NEG_FILL)
                m2 = jnp.where(offsets[2] == r, ml2[0, :, lanes2], NEG_FILL)
                top = jnp.maximum(m0, jnp.maximum(m1, m2))
                f0 = jnp.exp2(m0 - top)
                f1 = jnp.exp2(m1 - top)
                f2 = jnp.exp2(m2 - top)
                total = f0 * l[:, here] + f1 * ml1[s // 2, 1, :, lanes1] + f2 * ml2[1, :, lanes2]
                summed = f0 * o[:, here] + f1 * o1[s // 2, :, lanes1] + f2 * o2[:, lanes2]
                att = (summed / total).astype(BF16)
                attT[hh, r, :, lanes2] = att
                osta[0, hh, r, pl.ds(s * SRC0, SRC0)] = turn(att).reshape(SRC0, R, HD)
                lse[hh, r, :, lanes2] = top + jnp.log(total) * LOG2E
            return c

        lax.fori_loop(0, SEGS0, level0, 0)
        return carry

    lax.fori_loop(0, HPD, forward, 0)

    wait_bytes(recv_c.at[:, :, pl.ds(0, G - 1)], recv_sem.at[3])

    def gain_of(hh):
        g = gain[pl.ds(mine * HPD + hh, 1), :]
        return jnp.sum(jnp.where(eye_mask, g, 0.0), axis=1, keepdims=True)

    gains = [gain_of(hh) for hh in range(HPD)]
    for r in range(RES):
        sums = None
        for hh in range(HPD):
            a = attT[hh, r].astype(F32)
            cT = turn(recv_c[hh, r].reshape(LEN, HD))
            doT[hh, r] = cT
            dx = cT.astype(F32) * gains[hh]
            part = [jnp.sum(x, axis=0, keepdims=True) for x in (a, a * a, dx, dx * a)]
            sums = part if sums is None else [x + y for x, y in zip(sums, part)]
        for kind in range(4):
            part_sums[kind * RES + r] = sums[kind]

    def send_stats(i, c):
        peer = lax.rem(slot + i, NP)
        pltpu.make_async_remote_copy(
            src_ref=part_sums.at[pl.ds(lax.rem(peer, G) * ROWS, ROWS)],
            dst_ref=srecv.at[slot],
            send_sem=ssend_sem,
            recv_sem=srecv_sem,
            device_id={"ctx": base + lax.rem(peer, G), "head": peer // G},
            device_id_type=pl.DeviceIdType.MESH,
        ).start()
        return c

    lax.fori_loop(1, NP, send_stats, 0)
    srecv[slot] = part_sums[pl.ds(mine * ROWS, ROWS)]
    wait_bytes(srecv.at[pl.ds(0, NP - 1)], srecv_sem)
    own_rows = pl.ds(mine * ROWS, ROWS)
    sums_all[own_rows] = jnp.sum(srecv[...], axis=0)

    def send_sums(i, c):
        pltpu.make_async_remote_copy(
            src_ref=sums_all.at[own_rows],
            dst_ref=sums_all.at[own_rows],
            send_sem=gsend_sem,
            recv_sem=grecv_sem,
            device_id={"ctx": base + lax.rem(mine + i, G)},
            device_id_type=pl.DeviceIdType.MESH,
        ).start()
        return c

    lax.fori_loop(1, G, send_sums, 0)

    def send_att(i, c):
        d = lax.rem(mine + 7 * i, G)
        pltpu.make_async_remote_copy(
            src_ref=osta.at[0, :, :, d],
            dst_ref=rout.at[0, :, mine],
            send_sem=osend_sem.at[0],
            recv_sem=orecv_sem.at[0],
            device_id={"ctx": base + d},
            device_id_type=pl.DeviceIdType.MESH,
        ).start()
        return c

    lax.fori_loop(1, G, send_att, 0)
    own_att = pltpu.make_async_copy(osta.at[0, :, :, mine], rout.at[0, :, mine], own_sem.at[HPD])
    own_att.start()

    wait_bytes(sums_all.at[pl.ds(0, (G - 1) * ROWS)], grecv_sem)
    tot[...] = sums_all[...]

    inv_f = 1.0 / total_features
    for r in range(RES):
        mean = tot[r] * inv_f
        var = tot[RES + r] * inv_f - mean * mean
        inv = 1.0 / jnp.sqrt(var + EPSILON)
        s1 = tot[2 * RES + r]
        s2 = inv * (tot[3 * RES + r] - mean * s1)
        s1 = s1 * inv_f
        s2 = s2 * inv_f
        for hh in range(HPD):
            a = attT[hh, r].astype(F32)
            xhat = (a - mean) * inv
            dx = doT[hh, r].astype(F32) * gains[hh]
            d = ((dx - s1 - xhat * s2) * inv).astype(BF16)
            delta[hh, r] = jnp.sum(d.astype(F32) * a, axis=0, keepdims=True)
            doT[hh, r] = d
            n = SRC0
            for s in range(SEGS0):
                here = slice(s * W0, (s + 1) * W0)
                doN[hh, r, s * n:(s + 1) * n] = turn(d[:, here]).reshape(n, R, HD)

    def backward(hh, carry):
        offsets = [offset(level, hh) for level in range(LEVELS)]

        def segment(level, s):
            off = offsets[level]
            qn = n_pick(rows(0, hh), level, s, off)
            kn = n_pick(rows(1, hh), level, s, off)
            vn = n_pick(rows(2, hh), level, s, off)
            dn = n_pick(lambda r, d: doN[hh, r, d], level, s, off)
            dt = t_pick(lambda r, d: doT[hh, r, :, d], level, s, off)
            kt = t_pick(lambda r, d: kT[hh, r, :, d], level, s, off)
            ls = t_pick(lambda r, d: lse[hh, r, :, d], level, s, off)
            de = t_pick(lambda r, d: delta[hh, r, :, d], level, s, off)
            p = jnp.exp2(nt(kn, qn) * (SCALE * LOG2E) - ls)
            ds = (p * (nn(vn, dt) - de)).astype(BF16)
            return nn(kt, ds), nn(ds, qn), nn(p.astype(BF16), dn)

        dq2[...], dk2[...], dv2[...] = segment(2, 0)
        for s in range(2):
            dq1[s], dk1[s], dv1[s] = segment(1, s)
        w1 = [jnp.where(offsets[1] == r % 2, 1.0, 0.0).astype(F32) for r in range(RES)]
        w2 = [jnp.where(offsets[2] == r, 1.0, 0.0).astype(F32) for r in range(RES)]

        def level0(s, c):
            dq, dk, dv = segment(0, s)
            at2 = pl.ds(pl.multiple_of(s * W0, W0), W0)
            to = pl.ds(s * SRC0, SRC0)
            for r in range(RES):
                here = slice(r * W0, (r + 1) * W0)
                at1 = pl.ds(level1_at(s, r), W0)
                x = (dq[:, here] + w1[r] * dq1[s // 2, :, at1] + w2[r] * dq2[:, at2]) * SCALE
                osta[1, hh, r, to] = turn(x.astype(BF16)).reshape(SRC0, R, HD)
                x = (dk[here] + w1[r] * dk1[s // 2, at1] + w2[r] * dk2[at2]) * SCALE
                osta[2, hh, r, to] = x.astype(BF16).reshape(SRC0, R, HD)
                x = dv[here] + w1[r] * dv1[s // 2, at1] + w2[r] * dv2[at2]
                osta[3, hh, r, to] = x.astype(BF16).reshape(SRC0, R, HD)
            return c

        lax.fori_loop(0, SEGS0, level0, 0)

        def send(i, c):
            d = lax.rem(mine + 7 * i, G)
            pltpu.make_async_remote_copy(
                src_ref=osta.at[pl.ds(1, 3), hh, :, d],
                dst_ref=rout.at[pl.ds(1, 3), hh, mine],
                send_sem=osend_sem.at[1 + hh],
                recv_sem=orecv_sem.at[1 + hh],
                device_id={"ctx": base + d},
                device_id_type=pl.DeviceIdType.MESH,
            ).start()
            return c

        lax.fori_loop(1, G, send, 0)
        pltpu.make_async_copy(
            osta.at[pl.ds(1, 3), hh, :, mine], rout.at[pl.ds(1, 3), hh, mine], own_sem.at[hh]
        ).start()
        return carry

    lax.fori_loop(0, HPD, backward, 0)

    wait_bytes(rout.at[0, :, pl.ds(0, G - 1)], orecv_sem.at[0])
    own_att.wait()
    for hh in range(HPD):
        wait_bytes(rout.at[pl.ds(1, 3), hh, pl.ds(0, G - 1)], orecv_sem.at[1 + hh])
        pltpu.make_async_copy(
            osta.at[pl.ds(1, 3), hh, :, mine], rout.at[pl.ds(1, 3), hh, mine], own_sem.at[hh]
        ).wait()

    for a in range(4):
        wait_bytes(stage.at[a, pl.ds(0, G - 1)], send_sem.at[a])
    wait_bytes(srecv.at[pl.ds(0, NP - 1)], ssend_sem)
    wait_bytes(sums_all.at[pl.ds(0, (G - 1) * ROWS)], gsend_sem)
    wait_bytes(osta.at[0, :, :, pl.ds(0, G - 1)], osend_sem.at[0])
    for hh in range(HPD):
        wait_bytes(osta.at[pl.ds(1, 3), hh, :, pl.ds(0, G - 1)], osend_sem.at[1 + hh])


def finish(G, HPD, T, total_features, rout, tot, gain, n_out, dq_out, dk_out, dv_out):
    R = T // RES
    LEN = G * R
    mine = lax.rem(lax.axis_index("ctx"), G)
    ia = lax.broadcasted_iota(jnp.int32, (T, T), 0)
    ib = lax.broadcasted_iota(jnp.int32, (T, T), 1)
    perm_t = jnp.where(ia == lax.rem(ib, R) * RES + ib // R, 1.0, 0.0).astype(BF16)
    row = lax.broadcasted_iota(jnp.int32, (R, LEN), 0)
    lane = lax.broadcasted_iota(jnp.int32, (R, LEN), 1)
    own = lane == mine * R + row

    def column(kind):
        parts = [
            jnp.sum(jnp.where(own, tot[kind * RES + r], 0.0), axis=1, keepdims=True)
            for r in range(RES)
        ]
        return jnp.concatenate(parts, 0)

    inv_f = 1.0 / total_features
    mean = column(0) * inv_f
    var = column(1) * inv_f - mean * mean
    inv = 1.0 / jnp.sqrt(var + EPSILON)
    for g in range(0, rout.shape[2], 2):
        heads = [(g + j, hh) for j in range(2) for hh in range(HPD)]
        here = slice(g * HPD * HD, (g + 2) * HPD * HD)
        a = jnp.concatenate([rout[0, hh, j].reshape(T, HD) for j, hh in heads], 1).astype(F32)
        normed = ((a - mean) * inv * gain[:, here]).astype(BF16)
        n_out[:, here] = nn(perm_t, normed).astype(BF16)
        for k, ref in ((1, dq_out), (2, dk_out), (3, dv_out)):
            x = jnp.concatenate([rout[k, hh, j].reshape(T, HD) for j, hh in heads], 1)
            ref[:, here] = nn(perm_t, x).astype(BF16)


def on_device(queries, key_rows, value_rows, offsets, sublayer_norm_gain, cotangent):
    T, features = queries.shape
    heads = offsets.shape[1]
    NH = lax.axis_size("head")
    G = SEG0 * RES // T
    HPD = heads // G
    R = T // RES
    LEN = G * R
    NP = G * NH
    vm = pl.BlockSpec(memory_space=pltpu.VMEM)
    out = jax.ShapeDtypeStruct((T, features), BF16)
    big = pltpu.VMEM((4, HPD, RES, G, R, HD), BF16)
    scratch = [
        pltpu.VMEM((4, T, features), BF16),
        pltpu.VMEM((4, G, HPD, RES, R, HD), BF16),
        pltpu.VMEM((3, HPD, RES, G, R, HD), BF16),
        pltpu.VMEM((HPD, RES, G, R, HD), BF16),
        big,
        pltpu.VMEM((HPD, RES, HD, LEN), BF16),
        pltpu.VMEM((RES, HD, LEN), BF16),
        pltpu.VMEM((HPD, RES, HD, LEN), BF16),
        pltpu.VMEM((HPD, RES, HD, LEN), BF16),
        pltpu.VMEM((HPD, RES, G, R, HD), BF16),
        pltpu.VMEM((2, HD, SEG0), F32),
        pltpu.VMEM((2, 2, 1, SEG0), F32),
        pltpu.VMEM((HD, SEG0), F32),
        pltpu.VMEM((2, 1, SEG0), F32),
        pltpu.VMEM((2, HD, SEG0), F32),
        pltpu.VMEM((2, SEG0, HD), F32),
        pltpu.VMEM((2, SEG0, HD), F32),
        pltpu.VMEM((HD, SEG0), F32),
        pltpu.VMEM((SEG0, HD), F32),
        pltpu.VMEM((SEG0, HD), F32),
        pltpu.VMEM((HPD, RES, 1, LEN), F32),
        pltpu.VMEM((HPD, RES, 1, LEN), F32),
        pltpu.VMEM((4 * RES, 1, LEN), F32),
        pltpu.VMEM((NP, 4 * RES // G, 1, LEN), F32),
        pltpu.VMEM((4 * RES, 1, LEN), F32),
        pltpu.SemaphoreType.DMA((4,)),
        pltpu.SemaphoreType.DMA((1 + HPD,)),
        pltpu.SemaphoreType.DMA((4,)),
        pltpu.SemaphoreType.DMA((4,)),
        pltpu.SemaphoreType.DMA((1 + HPD,)),
        pltpu.SemaphoreType.DMA((1 + HPD,)),
        pltpu.SemaphoreType.DMA,
        pltpu.SemaphoreType.DMA,
        pltpu.SemaphoreType.DMA,
        pltpu.SemaphoreType.DMA,
    ]
    anywhere = pl.BlockSpec(memory_space=pl.ANY)
    total_features = float(NH * features)
    back, tot = pl.pallas_call(
        functools.partial(kernel, G, NH, HPD, T, total_features),
        out_shape=(
            jax.ShapeDtypeStruct((4, HPD, G, RES, R, HD), BF16),
            jax.ShapeDtypeStruct((4 * RES, 1, LEN), F32),
        ),
        in_specs=[pl.BlockSpec(memory_space=pltpu.SMEM), vm] + [anywhere] * 4,
        out_specs=(anywhere, vm),
        scratch_shapes=scratch,
        compiler_params=pltpu.CompilerParams(
            collective_id=0, has_side_effects=True, vmem_limit_bytes=58 * 2**20
        ),
        cost_estimate=pl.CostEstimate(
            flops=7_000_000_000, bytes_accessed=8 * 2**20, transcendentals=8_000_000
        ),
    )(offsets, sublayer_norm_gain.reshape(heads, HD), queries, key_rows, value_rows, cotangent)
    steps = min(4, G)
    width = features // steps
    return pl.pallas_call(
        functools.partial(finish, G, HPD, T, total_features),
        grid=(steps,),
        out_shape=(out,) * 4,
        in_specs=[
            pl.BlockSpec((4, HPD, G // steps, RES, R, HD), lambda i: (0, 0, i, 0, 0, 0)),
            pl.BlockSpec((4 * RES, 1, LEN), lambda i: (0, 0, 0)),
            pl.BlockSpec((1, width), lambda i: (0, i)),
        ],
        out_specs=(pl.BlockSpec((T, width), lambda i: (0, i)),) * 4,
        compiler_params=pltpu.CompilerParams(vmem_limit_bytes=58 * 2**20),
        cost_estimate=pl.CostEstimate(
            flops=8 * T * T * features, bytes_accessed=8 * 2**20, transcendentals=0
        ),
    )(back, tot, sublayer_norm_gain.reshape(1, features))


def solution(mesh):
    spec = P("ctx", "head")
    return jax.shard_map(
        on_device,
        mesh=mesh,
        in_specs=(spec, spec, spec, P(None, "head"), P("head"), spec),
        out_specs=(spec,) * 4,
        check_vma=False,
    )
```
